32 devices in a mesh: space: 4 (over z), tp: 8 (over y, x, core).
Axes of the slice: x: 2, y: 2, z: 4, core: 2. Of those that a mesh axis runs over, the one named last changes fastest.
Arguments:
- queries: bfloat16 [32, 32, 4, 1024], P('space', 'tp'), may hold values from -9.7 to 9.7
- key_field: bfloat16 [32, 32, 4, 1024], P('space', 'tp'), may hold values from -4 to 4
- value_field: bfloat16 [32, 32, 4, 1024], P('space', 'tp'), may hold values from -12 to 12
- upstream: bfloat16 [32, 32, 4, 1024], P('space', 'tp'), may hold values from -6 to 6
Outputs:
- out: bfloat16 [32, 32, 4, 1024], P('space', 'tp')
- grad_queries: bfloat16 [32, 32, 4, 1024], P('space', 'tp')
- grad_keys: bfloat16 [32, 32, 4, 1024], P('space', 'tp')
- grad_values: bfloat16 [32, 32, 4, 1024], P('space', 'tp')
The draws below stay inside these ranges and needn't reach their ends.
All inputs are finite; a program needn't handle non-finite values.
Results may differ from the reference program's by a relative error of at most 0.0093.
Values may be sent and summed in bfloat16 or wider, within the bound.
A program may use at most 64 MiB of HBM per device.

```python
import math
import jax
import jax.numpy as jnp
from jax import lax

D = 1024
HEADS = 16
RADIUS = 3
CX = 8
CY = 4
GZ = 4
GX = 32
GY = 32


def draw_queries(key, part):
    drawn = jax.random.truncated_normal(jax.random.fold_in(key, 11), -4.0, 4.0, (GX, GY, GZ, D), jnp.float32)
    return drawn.astype(jnp.bfloat16)


def draw_key_field(key, part):
    drawn = jax.random.truncated_normal(jax.random.fold_in(key, 13), -4.0, 4.0, (GX, GY, GZ, D), jnp.float32)
    return drawn.astype(jnp.bfloat16)


def steps_of(rng, shape, shards, low, top_value):
    gain, own = 1.0, jax.random.fold_in(rng, 6)
    for dim, shards_of in shards:
        heights = jnp.exp(jax.random.uniform(jax.random.fold_in(own, dim), (shards_of,), jnp.float32, low / len(shards), top_value / len(shards)))
        gain = gain * jnp.repeat(heights, shape[dim] // shards_of).reshape([-1 if axis == dim else 1 for axis in range(len(shape))])
    return gain


def scatter_about(rng, shape, width, bound, shards=(), kind=jnp.bfloat16):
    entries = width * jax.random.normal(rng, shape, jnp.float32)
    if shards:
        entries = entries * steps_of(rng, shape, shards, -0.22, 0.18)
    return jnp.clip(entries, -bound, bound).astype(kind)


def setup_inputs(seed: int = 0) -> dict:
    arg_keys = jax.random.split(jax.random.key(seed), 5)
    return {
        "queries": draw_queries(jax.random.fold_in(arg_keys[4], 71), 0),
        "key_field": draw_key_field(jax.random.fold_in(arg_keys[4], 71), 0),
        "value_field": scatter_about(arg_keys[2], (GX, GY, GZ, D), 2.0, 12.0, ((0, 4), (1, 8))),
        "upstream": scatter_about(arg_keys[3], (GX, GY, GZ, D), 1.0, 6.0, ((0, 4), (1, 8))),
    }


blocked_score = -1e+30
heads_group = 4

def window_mask(along_x, along_y, depth_z, first_x, first_y, grid_x, grid_y, rim_width):
    centre_x, centre_y, centre_z = jnp.meshgrid(jnp.arange(along_x, dtype=jnp.int32), jnp.arange(along_y, dtype=jnp.int32), jnp.arange(depth_z, dtype=jnp.int32), indexing='ij')
    other_x, other_y, other_z = jnp.meshgrid(jnp.arange(along_x + 2 * rim_width, dtype=jnp.int32), jnp.arange(along_y + 2 * rim_width, dtype=jnp.int32), jnp.arange(depth_z, dtype=jnp.int32), indexing='ij')
    centre_x = centre_x.reshape(-1)[:, None]
    centre_y = centre_y.reshape(-1)[:, None]
    centre_z = centre_z.reshape(-1)[:, None]
    other_x = other_x.reshape(-1)[None, :]
    other_y = other_y.reshape(-1)[None, :]
    other_z = other_z.reshape(-1)[None, :]
    within = (jnp.abs(other_x - centre_x - rim_width) <= rim_width) & (jnp.abs(other_y - centre_y - rim_width) <= rim_width) & (jnp.abs(other_z - centre_z) <= rim_width)
    global_x = first_x + other_x - rim_width
    global_y = first_y + other_y - rim_width
    inside = (global_x >= 0) & (global_x < grid_x) & (global_y >= 0) & (global_y < grid_y)
    return within & inside

def take_heads(matrix, group_index, group_width):
    part = lax.dynamic_slice_in_dim(matrix, group_index * group_width, group_width, 1)
    return part.reshape(matrix.shape[0], heads_group, -1).astype(jnp.float32)

def take_stats(matrix, group_index):
    return jnp.transpose(lax.dynamic_slice_in_dim(matrix, group_index * heads_group, heads_group, 1))

def regroup(stacked):
    groups, row_total, group_width = stacked.shape
    return jnp.transpose(stacked, (1, 0, 2)).reshape(row_total, groups * group_width)

def regroup_heads(stacked):
    groups, per_group, row_total = stacked.shape
    return jnp.transpose(stacked, (2, 0, 1)).reshape(row_total, groups * per_group)

def rounded(values_in):
    return lax.optimization_barrier(values_in.astype(jnp.bfloat16)).astype(jnp.float32)

def attend_forward(centre_q, other_k, other_v, allowed, head_size):
    row_total = centre_q.shape[0]
    group_width = heads_group * head_size
    inv_root = 1.0 / math.sqrt(head_size)

    def one_group(group_index):
        query_part = take_heads(centre_q, group_index, group_width)
        key_part = take_heads(other_k, group_index, group_width)
        value_part = take_heads(other_v, group_index, group_width)
        scores = jnp.einsum('qhd,khd->hqk', query_part, key_part) * inv_root
        scores = jnp.where(allowed[None], scores, blocked_score)
        highest = lax.optimization_barrier(jnp.max(scores, axis=2, keepdims=True))
        summed = lax.optimization_barrier(jnp.sum(jnp.exp(scores - highest), axis=2, keepdims=True))
        log_total = highest + jnp.log(summed)
        weights = rounded(jnp.exp(scores - log_total))
        attended = jnp.einsum('hqk,khd->qhd', weights, value_part).astype(jnp.bfloat16)
        return (attended.reshape(row_total, group_width), log_total[:, :, 0])
    attended, log_total = lax.map(one_group, jnp.arange(HEADS // heads_group, dtype=jnp.int32))
    return (regroup(attended), regroup_heads(log_total))

def attend_queries(centre_q, centre_up, centre_lse, centre_dots, other_k, other_v, allowed, head_size):
    row_total = centre_q.shape[0]
    group_width = heads_group * head_size
    inv_root = 1.0 / math.sqrt(head_size)

    def one_group(group_index):
        up_part = take_heads(centre_up, group_index, group_width)
        query_part = take_heads(centre_q, group_index, group_width)
        key_part = take_heads(other_k, group_index, group_width)
        value_part = take_heads(other_v, group_index, group_width)
        lse_part = take_stats(centre_lse, group_index)
        dot_part = take_stats(centre_dots, group_index)
        scores = jnp.einsum('qhd,khd->hqk', query_part, key_part) * inv_root
        scores = jnp.where(allowed[None], scores, blocked_score)
        exact_prob = jnp.exp(scores - lse_part[:, :, None])
        d_prob = jnp.einsum('qhd,khd->hqk', up_part, value_part)
        dscore = rounded(exact_prob * (d_prob - dot_part[:, :, None]))
        grad_q = (jnp.einsum('hqk,khd->qhd', dscore, key_part) * inv_root).astype(jnp.bfloat16)
        return grad_q.reshape(row_total, group_width)
    return regroup(lax.map(one_group, jnp.arange(HEADS // heads_group, dtype=jnp.int32)))

def attend_keys(centre_k, centre_v, other_q, other_up, other_lse, other_dots, allowed, head_size):
    row_total = centre_k.shape[0]
    group_width = heads_group * head_size
    inv_root = 1.0 / math.sqrt(head_size)

    def one_group(group_index):
        key_part = take_heads(centre_k, group_index, group_width)
        value_part = take_heads(centre_v, group_index, group_width)
        query_part = take_heads(other_q, group_index, group_width)
        up_part = take_heads(other_up, group_index, group_width)
        lse_part = take_stats(other_lse, group_index)
        dot_part = take_stats(other_dots, group_index)
        scores = jnp.einsum('khd,qhd->hkq', key_part, query_part) * inv_root
        scores = jnp.where(allowed[None], scores, blocked_score)
        exact_prob = jnp.exp(scores - lse_part[:, None, :])
        weights = rounded(exact_prob)
        d_prob = jnp.einsum('khd,qhd->hkq', value_part, up_part)
        dscore = rounded(exact_prob * (d_prob - dot_part[:, None, :]))
        grad_k = (jnp.einsum('hkq,qhd->khd', dscore, query_part) * inv_root).astype(jnp.bfloat16)
        grad_v = jnp.einsum('hkq,qhd->khd', weights, up_part).astype(jnp.bfloat16)
        return (grad_k.reshape(row_total, group_width), grad_v.reshape(row_total, group_width))
    grad_k, grad_v = lax.map(one_group, jnp.arange(HEADS // heads_group, dtype=jnp.int32))
    return (regroup(grad_k), regroup(grad_v))

def head_products(flat_up, attended, head_count):
    fixed = lax.optimization_barrier(attended).astype(jnp.float32)
    product = flat_up.astype(jnp.float32) * fixed
    return product.reshape(product.shape[0], head_count, -1).sum(axis=2)

def reference(queries, key_field, value_field, upstream):
    grid_x, grid_y, depth_z, features = queries.shape
    head_size = features // HEADS
    blocks_x = grid_x // CX
    blocks_y = grid_y // CY
    span_x = CX + 2 * RADIUS
    span_y = CY + 2 * RADIUS
    row_total = CX * CY * depth_z
    others = span_x * span_y * depth_z
    padding = ((RADIUS, RADIUS), (RADIUS, RADIUS), (0, 0), (0, 0))

    def corner(block_id):
        start_x = (block_id // blocks_y).astype(jnp.int32) * CX
        start_y = (block_id % blocks_y).astype(jnp.int32) * CY
        return (start_x, start_y)

    def centre_of(field, block_id):
        start_x, start_y = corner(block_id)
        zero = jnp.zeros((), jnp.int32)
        piece_out = lax.dynamic_slice(field, (start_x, start_y, zero, zero), (CX, CY, depth_z, field.shape[3]))
        return piece_out.reshape(row_total, field.shape[3])

    def beside_all(padded, block_id):
        start_x, start_y = corner(block_id)
        zero = jnp.zeros((), jnp.int32)
        piece_out = lax.dynamic_slice(padded, (start_x, start_y, zero, zero), (span_x, span_y, depth_z, padded.shape[3]))
        return piece_out.reshape(others, padded.shape[3])

    def block_mask(block_id):
        start_x, start_y = corner(block_id)
        return window_mask(CX, CY, depth_z, start_x, start_y, grid_x, grid_y, RADIUS)

    def assemble(stacked):
        last_dim = stacked.shape[-1]
        shaped = stacked.reshape(blocks_x, blocks_y, CX, CY, depth_z, last_dim)
        return jnp.transpose(shaped, (0, 2, 1, 3, 4, 5)).reshape(grid_x, grid_y, depth_z, last_dim)
    block_ids = jnp.arange(blocks_x * blocks_y, dtype=jnp.int32)
    padded_k = jnp.pad(key_field, padding)
    padded_v = jnp.pad(value_field, padding)

    def forward_block(block_id):
        return attend_forward(centre_of(queries, block_id), beside_all(padded_k, block_id), beside_all(padded_v, block_id), block_mask(block_id), head_size)
    attended, log_total = lax.map(forward_block, block_ids)
    out = assemble(attended)
    lse_field = assemble(log_total)
    dot_field = head_products(upstream.reshape(-1, features), out.reshape(-1, features), HEADS).reshape(grid_x, grid_y, depth_z, HEADS)

    def query_block(block_id):
        return attend_queries(centre_of(queries, block_id), centre_of(upstream, block_id), centre_of(lse_field, block_id), centre_of(dot_field, block_id), beside_all(padded_k, block_id), beside_all(padded_v, block_id), block_mask(block_id), head_size)
    grad_queries = assemble(lax.map(query_block, block_ids))
    padded_q = jnp.pad(queries, padding)
    padded_up = jnp.pad(upstream, padding)
    padded_lse = jnp.pad(lse_field, padding)
    padded_dots = jnp.pad(dot_field, padding)

    def key_block(block_id):
        return attend_keys(centre_of(key_field, block_id), centre_of(value_field, block_id), beside_all(padded_q, block_id), beside_all(padded_up, block_id), beside_all(padded_lse, block_id), beside_all(padded_dots, block_id), block_mask(block_id), head_size)
    grad_k, grad_v = lax.map(key_block, block_ids)
    return (out, grad_queries, assemble(grad_k), assemble(grad_v))
```

```python
import functools

import jax
import jax.numpy as jnp
from jax import lax
from jax.experimental import pallas as pl
from jax.experimental.pallas import tpu as pltpu
from jax.sharding import PartitionSpec as P

HEADS = 16
RADIUS = 3
BLOCKED = -1e30
MESH = pl.DeviceIdType.MESH
NT = (((1,), (1,)), ((), ()))
TN = (((0,), (0,)), ((), ()))
NN = (((1,), (0,)), ((), ()))


def mm(a, b, dims):
    return lax.dot_general(a, b, dims, preferred_element_type=jnp.float32)


def kernel(
    ns, nt, q_ref, k_ref, v_ref, u_ref, o_ref, gq_ref, gk_ref, gv_ref,
    kv, bias, acc, zs, zr, ys, yr,
    ym_s, ym_r, z_s, z_r, zg_s, zg_r, yg_s, yg_r,
):
    G = kv.shape[0]
    si = lax.axis_index("space")
    ti = lax.axis_index("tp")
    has_lo, has_hi = si > 0, si < ns - 1
    has_l, has_r = ti > 0, ti < nt - 1
    lo, hi, left, right = (si - 1, ti), (si + 1, ti), (si, ti - 1), (si, ti + 1)

    barrier = pltpu.get_barrier_semaphore()
    for have, dev in ((has_lo, lo), (has_hi, hi), (has_l, left), (has_r, right)):
        @pl.when(have)
        def _(dev=dev):
            pl.semaphore_signal(barrier, inc=1, device_id=dev, device_id_type=MESH)

    def remote(src, dst, ss, rs, dev):
        return pltpu.make_async_remote_copy(
            src_ref=src, dst_ref=dst, send_sem=ss, recv_sem=rs, device_id=dev, device_id_type=MESH
        )

    def ymain(g):
        return (
            (remote(kv.at[g, :, 0:3, 0:2], kv.at[g, :, 7:10, 0:2], ym_s.at[g, 0], ym_r.at[g, 0], left), has_l, has_r),
            (remote(kv.at[g, :, 1:4, 0:2], kv.at[g, :, 4:7, 0:2], ym_s.at[g, 1], ym_r.at[g, 1], right), has_r, has_l),
        )

    def zmain(g):
        return (
            (remote(kv.at[g, :, :, 0], kv.at[g, :, :, 3], z_s.at[g, 0], z_r.at[g, 0], lo), has_lo, has_hi),
            (remote(kv.at[g, :, :, 1], kv.at[g, :, :, 2], z_s.at[g, 1], z_r.at[g, 1], hi), has_hi, has_lo),
        )

    def zgrad(g):
        return (
            (remote(zs.at[g, 0], zr.at[g, 0], zg_s.at[g, 0], zg_r.at[g, 0], lo), has_lo, has_hi),
            (remote(zs.at[g, 1], zr.at[g, 1], zg_s.at[g, 1], zg_r.at[g, 1], hi), has_hi, has_lo),
        )

    def ygrad(g):
        return (
            (remote(ys.at[g, 0], yr.at[g, 0], yg_s.at[g, 0], yg_r.at[g, 0], left), has_l, has_r),
            (remote(ys.at[g, 1], yr.at[g, 1], yg_s.at[g, 1], yg_r.at[g, 1], right), has_r, has_l),
        )

    def start(copies):
        for c, send, _r in copies:
            @pl.when(send)
            def _(c=c):
                c.start()

    def got(copies):
        for c, _s, recv in copies:
            @pl.when(recv)
            def _(c=c):
                c.wait_recv()

    def sent(copies):
        for c, send, _r in copies:
            @pl.when(send)
            def _(c=c):
                c.wait_send()

    def lanes(g):
        return pl.ds(pl.multiple_of(g * 128, 128), 128)

    r = lax.broadcasted_iota(jnp.int32, (128, 128), 0)
    c = lax.broadcasted_iota(jnp.int32, (128, 128), 1)
    want = ((r // 4) % 8) * 16 + (r // 32) * 4 + r % 4
    perm = jnp.where(c == want, 1.0, 0.0).astype(jnp.bfloat16)

    barrier_count = (
        has_lo.astype(jnp.int32) + has_hi.astype(jnp.int32) + has_l.astype(jnp.int32) + has_r.astype(jnp.int32)
    )

    def fill(g):
        for i, ref in enumerate((k_ref, v_ref)):
            own = mm(perm, ref[:, lanes(g)], NN).astype(jnp.bfloat16)
            kv[g, i, 0:4, 0:2] = own.reshape(4, 2, 16, 128)

    fill(0)
    pl.semaphore_wait(barrier, barrier_count)
    start(ymain(0))

    def prologue(g, carry):
        fill(g)
        start(ymain(g))
        return carry

    lax.fori_loop(1, G, prologue, 0)

    @pl.when(jnp.logical_not(has_l))
    def _():
        kv[:, :, 4:7, 0:2] = jnp.zeros((G, 2, 3, 2, 16, 128), jnp.bfloat16)

    @pl.when(jnp.logical_not(has_r))
    def _():
        kv[:, :, 7:10, 0:2] = jnp.zeros((G, 2, 3, 2, 16, 128), jnp.bfloat16)

    @pl.when(jnp.logical_not(has_lo))
    def _():
        kv[:, :, :, 2] = jnp.zeros((G, 2, 10, 16, 128), jnp.bfloat16)

    @pl.when(jnp.logical_not(has_hi))
    def _():
        kv[:, :, :, 3] = jnp.zeros((G, 2, 10, 16, 128), jnp.bfloat16)

    row = lax.broadcasted_iota(jnp.int32, (640, 128), 0)
    col = lax.broadcasted_iota(jnp.int32, (640, 128), 1)
    j, b, xi = row // 64, (row // 16) % 4, (row // 4) % 4
    ky = jnp.where(j < 4, j, jnp.where(j < 7, j - 7, j - 3))
    kx = jnp.where(b < 2, b * 4 + xi, jnp.where(b == 2, xi - 4, xi + 8))
    qx, qy = col // 16, (col // 4) % 4
    gx, gy = kx + si * 8, ky + ti * 4
    ok = (
        (jnp.abs(kx - qx) <= RADIUS) & (jnp.abs(ky - qy) <= RADIUS)
        & (gx >= 0) & (gx < ns * 8) & (gy >= 0) & (gy < nt * 4)
    )
    one = jnp.where(ok, 0.0, BLOCKED)
    bias[:, 0:128] = one
    bias[:, 128:256] = one

    lane = lax.broadcasted_iota(jnp.int32, (128, 128), 1)
    feat = lax.broadcasted_iota(jnp.int32, (128, 128), 0)

    def stacked(x):
        zero = jnp.zeros_like(x)
        return jnp.concatenate([jnp.where(lane < 64, x, zero), jnp.where(lane >= 64, x, zero)], axis=0).astype(jnp.bfloat16)

    def diagonal(x):
        return jnp.where(feat < 64, x[:, 0:128], x[:, 128:256])

    def forward(g):
        got(ymain(g))
        start(zmain(g))

    def compute(g):
        k = kv[g, 0].reshape(640, 128)
        v = kv[g, 1].reshape(640, 128)
        qf = q_ref[:, lanes(g)].astype(jnp.float32) * 0.125
        uf = u_ref[:, lanes(g)].astype(jnp.float32)
        qst, ust = stacked(qf), stacked(uf)
        s = mm(k, qst, NT) + bias[...]
        p = jnp.exp(s - jnp.max(s, axis=0, keepdims=True))
        w = p * (1.0 / jnp.sum(p, axis=0, keepdims=True))
        wb = w.astype(jnp.bfloat16)
        ot = diagonal(mm(v, wb, TN))
        o_ref[:, lanes(g)] = ot.T.astype(jnp.bfloat16)
        prod = uf.T * ot.astype(jnp.bfloat16).astype(jnp.float32)
        dots = jnp.concatenate(
            [jnp.sum(prod[0:64], axis=0, keepdims=True), jnp.sum(prod[64:128], axis=0, keepdims=True)], axis=1
        )
        ds = (w * (mm(v, ust, NT) - dots)).astype(jnp.bfloat16)
        gq_ref[:, lanes(g)] = (diagonal(mm(k, ds, TN)).T * 0.125).astype(jnp.bfloat16)
        for i, grad in enumerate((mm(ds, qst, NN), mm(wb, ust, NN))):
            grad = grad.reshape(10, 4, 16, 128)
            acc[g, i] = grad[:, 0:2]
            zs[g, 0, i] = grad[:, 2].astype(jnp.bfloat16)
            zs[g, 1, i] = grad[:, 3].astype(jnp.bfloat16)

    def stage_y(g):
        got(zgrad(g))

        @pl.when(has_hi)
        def _():
            acc[g, :, :, 1] += zr[g, 0].astype(jnp.float32)

        @pl.when(has_lo)
        def _():
            acc[g, :, :, 0] += zr[g, 1].astype(jnp.float32)

        ys[g, 0] = acc[g, :, 4:7].astype(jnp.bfloat16)
        ys[g, 1] = acc[g, :, 7:10].astype(jnp.bfloat16)
        start(ygrad(g))

    def stage_out(g):
        got(ygrad(g))

        @pl.when(has_r)
        def _():
            acc[g, :, 1:4] += yr[g, 0].astype(jnp.float32)

        @pl.when(has_l)
        def _():
            acc[g, :, 0:3] += yr[g, 1].astype(jnp.float32)

        for i, ref in enumerate((gk_ref, gv_ref)):
            own = acc[g, i, 0:4].reshape(128, 128).astype(jnp.bfloat16)
            ref[:, lanes(g)] = mm(perm, own, TN).astype(jnp.bfloat16)

    AHEAD = 2
    for g in range(AHEAD):
        forward(g)

    def step(g, carry):
        @pl.when(g + AHEAD < G)
        def _():
            forward(g + AHEAD)

        @pl.when(g < G)
        def _():
            got(zmain(g))
            compute(g)
            start(zgrad(g))

        @pl.when((g >= 1) & (g < G + 1))
        def _():
            stage_y(g - 1)

        @pl.when(g >= 3)
        def _():
            stage_out(g - 3)

        return carry

    lax.fori_loop(0, G + 3, step, 0)

    def drain(g, carry):
        for copies in (ymain(g), zmain(g), zgrad(g), ygrad(g)):
            sent(copies)
        return carry

    lax.fori_loop(0, G, drain, 0)


def on_device(queries, key_field, value_field, upstream):
    shape = queries.shape
    rows, feats = shape[0] * shape[1] * shape[2], shape[3]
    pairs = feats // 128
    flat = [x.reshape(rows, feats) for x in (queries, key_field, value_field, upstream)]
    vmem = pl.BlockSpec(memory_space=pltpu.VMEM)
    dma = lambda: pltpu.SemaphoreType.DMA((pairs, 2))
    outs = pl.pallas_call(
        functools.partial(kernel, lax.axis_size("space"), lax.axis_size("tp")),
        out_shape=[jax.ShapeDtypeStruct((rows, feats), jnp.bfloat16)] * 4,
        in_specs=[vmem] * 4,
        out_specs=[vmem] * 4,
        scratch_shapes=[
            pltpu.VMEM((pairs, 2, 10, 4, 16, 128), jnp.bfloat16),
            pltpu.VMEM((640, 256), jnp.float32),
            pltpu.VMEM((pairs, 2, 10, 2, 16, 128), jnp.float32),
            pltpu.VMEM((pairs, 2, 2, 10, 16, 128), jnp.bfloat16),
            pltpu.VMEM((pairs, 2, 2, 10, 16, 128), jnp.bfloat16),
            pltpu.VMEM((pairs, 2, 2, 3, 2, 16, 128), jnp.bfloat16),
            pltpu.VMEM((pairs, 2, 2, 3, 2, 16, 128), jnp.bfloat16),
        ] + [dma() for _ in range(8)],
        compiler_params=pltpu.CompilerParams(
            collective_id=0, has_side_effects=True, vmem_limit_bytes=48 * 1024 * 1024
        ),
        cost_estimate=pl.CostEstimate(flops=2 * 10**9, bytes_accessed=4 * 10**6, transcendentals=10**6),
        name="window_attention",
    )(*flat)
    return tuple(x.reshape(shape) for x in outs)


def solution(mesh):
    spec = P("space", "tp", None, None)
    return jax.shard_map(
        on_device, mesh=mesh, in_specs=(spec,) * 4, out_specs=(spec,) * 4, check_vma=False
    )
```

```python
import functools

import jax
import jax.numpy as jnp
from jax import lax
from jax.experimental import pallas as pl
from jax.experimental.pallas import tpu as pltpu
from jax.sharding import PartitionSpec as P

HEADS = 16
RADIUS = 3
BLOCKED = -1e30
MESH = pl.DeviceIdType.MESH
NT = (((1,), (1,)), ((), ()))
TN = (((0,), (0,)), ((), ()))
NN = (((1,), (0,)), ((), ()))


def mm(a, b, dims):
    return lax.dot_general(a, b, dims, preferred_element_type=jnp.float32)


def kernel(
    ns, nt, q_ref, k_ref, v_ref, u_ref, o_ref, gq_ref, gk_ref, gv_ref,
    kv, pack, rim, kmask, qmask, acc, zs, zr, ys, yr,
    ym_s, ym_r, z_s, z_r, zg_s, zg_r, yg_s, yg_r,
):
    G = kv.shape[0]
    si = lax.axis_index("space")
    ti = lax.axis_index("tp")
    has_lo, has_hi = si > 0, si < ns - 1
    has_l, has_r = ti > 0, ti < nt - 1
    lo, hi, left, right = (si - 1, ti), (si + 1, ti), (si, ti - 1), (si, ti + 1)

    barrier = pltpu.get_barrier_semaphore()
    for have, dev in ((has_lo, lo), (has_hi, hi), (has_l, left), (has_r, right)):
        @pl.when(have)
        def _(dev=dev):
            pl.semaphore_signal(barrier, inc=1, device_id=dev, device_id_type=MESH)

    def remote(src, dst, ss, rs, dev):
        return pltpu.make_async_remote_copy(
            src_ref=src, dst_ref=dst, send_sem=ss, recv_sem=rs, device_id=dev, device_id_type=MESH
        )

    def ymain(g):
        return (
            (remote(kv.at[g, :, 0:3], kv.at[g, :, 7:10], ym_s.at[g, 0], ym_r.at[g, 0], left), has_l, has_r),
            (remote(kv.at[g, :, 1:4], kv.at[g, :, 4:7], ym_s.at[g, 1], ym_r.at[g, 1], right), has_r, has_l),
        )

    def zmain(g):
        return (
            (remote(pack.at[g, 0], rim.at[g, 1], z_s.at[g, 0], z_r.at[g, 0], lo), has_lo, has_hi),
            (remote(pack.at[g, 1], rim.at[g, 0], z_s.at[g, 1], z_r.at[g, 1], hi), has_hi, has_lo),
        )

    def zgrad(g):
        return (
            (remote(zs.at[g, 0], zr.at[g, 0], zg_s.at[g, 0], zg_r.at[g, 0], lo), has_lo, has_hi),
            (remote(zs.at[g, 1], zr.at[g, 1], zg_s.at[g, 1], zg_r.at[g, 1], hi), has_hi, has_lo),
        )

    def ygrad(g):
        return (
            (remote(ys.at[g, 0], yr.at[g, 0], yg_s.at[g, 0], yg_r.at[g, 0], left), has_l, has_r),
            (remote(ys.at[g, 1], yr.at[g, 1], yg_s.at[g, 1], yg_r.at[g, 1], right), has_r, has_l),
        )

    def start(copies):
        for c, send, _r in copies:
            @pl.when(send)
            def _(c=c):
                c.start()

    def got(copies):
        for c, _s, recv in copies:
            @pl.when(recv)
            def _(c=c):
                c.wait_recv()

    def sent(copies):
        for c, send, _r in copies:
            @pl.when(send)
            def _(c=c):
                c.wait_send()

    def lanes(g):
        return pl.ds(pl.multiple_of(g * 128, 128), 128)

    r = lax.broadcasted_iota(jnp.int32, (128, 128), 0)
    c = lax.broadcasted_iota(jnp.int32, (128, 128), 1)
    want = ((r // 4) % 8) * 16 + (r // 32) * 4 + r % 4
    perm = jnp.where(c == want, 1.0, 0.0).astype(jnp.bfloat16)

    barrier_count = (
        has_lo.astype(jnp.int32) + has_hi.astype(jnp.int32) + has_l.astype(jnp.int32) + has_r.astype(jnp.int32)
    )

    def choose(packed, cell, first):
        hit = (cell == (packed // 12) * 16 + packed % 12 + first) & (packed < 120)
        return jnp.where(hit, 1.0, 0.0).astype(jnp.bfloat16)

    def iota(shape, dim):
        return lax.broadcasted_iota(jnp.int32, shape, dim)

    packs = [choose(iota((128, 160), 0), iota((128, 160), 1), 4 * i) for i in range(2)]
    unpacks = [choose(iota((160, 128), 1), iota((160, 128), 0), 4 * i) for i in range(2)]

    def cells(ref, g):
        return ref[:, :, :, lanes(g)].astype(jnp.float32).reshape(128, 128)

    def put(ref, g, x):
        ref[:, :, :, lanes(g)] = x.reshape(8, 4, 4, 128).astype(jnp.bfloat16)

    def fill(g):
        for i, ref in enumerate((k_ref, v_ref)):
            own = mm(perm, cells(ref, g).astype(jnp.bfloat16), NN).astype(jnp.bfloat16)
            kv[g, i, 0:4] = own.reshape(4, 2, 16, 128)

    fill(0)
    pl.semaphore_wait(barrier, barrier_count)
    start(ymain(0))

    def prologue(g, carry):
        fill(g)
        start(ymain(g))
        return carry

    lax.fori_loop(1, G, prologue, 0)

    @pl.when(jnp.logical_not(has_l))
    def _():
        kv[:, :, 4:7] = jnp.zeros((G, 2, 3, 2, 16, 128), jnp.bfloat16)

    @pl.when(jnp.logical_not(has_r))
    def _():
        kv[:, :, 7:10] = jnp.zeros((G, 2, 3, 2, 16, 128), jnp.bfloat16)

    @pl.when(jnp.logical_not(has_lo))
    def _():
        rim[:, 0] = jnp.zeros((G, 2, 128, 128), jnp.bfloat16)

    @pl.when(jnp.logical_not(has_hi))
    def _():
        rim[:, 1] = jnp.zeros((G, 2, 128, 128), jnp.bfloat16)

    row, f = iota((576, 128), 0), iota((576, 128), 1)
    low, high = row < 128, row >= 448
    t = jnp.where(low, row, jnp.where(high, row - 448, row - 128))
    edge = low | high
    j = jnp.where(edge, t // 12, t // 32)
    spare = edge & (t >= 120)
    ky = jnp.where(j < 4, j, jnp.where(j < 7, j - 7, j - 3))
    kx = jnp.where(low, (t % 12) // 4 - 3, jnp.where(high, (t % 12) // 4 + 8, (t % 32) // 4))
    on = (spare & (f == 32)) | (jnp.logical_not(spare) & ((f == kx + 3) | (f == ky + 19)))
    kmask[...] = jnp.where(on, 1.0, 0.0).astype(jnp.bfloat16)

    col, f = iota((256, 128), 0) % 128, iota((256, 128), 1)
    qx, qy = col // 16, (col // 4) % 4
    kx, ky = f - 3, f - 19
    gx, gy = kx + si * 8, ky + ti * 4
    far_x = (jnp.abs(kx - qx) > RADIUS) | (gx < 0) | (gx >= ns * 8)
    far_y = (jnp.abs(ky - qy) > RADIUS) | (gy < 0) | (gy >= nt * 4)
    off = ((f < 14) & far_x) | ((f >= 16) & (f < 26) & far_y) | (f == 32)
    qmask[...] = jnp.where(off, BLOCKED, 0.0).astype(jnp.bfloat16)

    lane = lax.broadcasted_iota(jnp.int32, (128, 128), 1)
    feat = lax.broadcasted_iota(jnp.int32, (128, 128), 0)

    def stacked(x):
        zero = jnp.zeros_like(x)
        return jnp.concatenate([jnp.where(lane < 64, x, zero), jnp.where(lane >= 64, x, zero)], axis=0).astype(jnp.bfloat16)

    def diagonal(x):
        return jnp.where(feat < 64, x[:, 0:128], x[:, 128:256])

    def forward(g):
        got(ymain(g))
        for i in range(2):
            both = jnp.concatenate([kv[g, 0, :, i].reshape(160, 128), kv[g, 1, :, i].reshape(160, 128)], axis=1)
            out = mm(packs[i], both, NN).astype(jnp.bfloat16)
            pack[g, i, 0] = out[:, 0:128]
            pack[g, i, 1] = out[:, 128:256]
        start(zmain(g))

    def compute(g):
        def all_rows(i):
            return jnp.concatenate([rim[g, 0, i], kv[g, i].reshape(320, 128), rim[g, 1, i]], axis=0)

        k, v = all_rows(0), all_rows(1)
        qf, uf = cells(q_ref, g) * 0.125, cells(u_ref, g)
        s = mm(
            jnp.concatenate([k, kmask[...]], axis=1), jnp.concatenate([stacked(qf), qmask[...]], axis=1), NT
        )
        p = jnp.exp(s - jnp.max(s, axis=0, keepdims=True))
        inv = 1.0 / jnp.sum(p, axis=0, keepdims=True)
        inv = jnp.where(feat < 64, inv[:, 0:128], inv[:, 128:256])
        pb = p.astype(jnp.bfloat16)
        ot = diagonal(mm(v, pb, TN)) * inv
        put(o_ref, g, ot.T)
        prod = uf.T * ot.astype(jnp.bfloat16).astype(jnp.float32)
        dots = jnp.concatenate(
            [jnp.sum(prod[0:64], axis=0, keepdims=True), jnp.sum(prod[64:128], axis=0, keepdims=True)], axis=1
        )
        ds = (p * (mm(v, stacked(uf), NT) - dots)).astype(jnp.bfloat16)
        put(gq_ref, g, (diagonal(mm(k, ds, TN)) * (inv * 0.125)).T)
        inv = inv.T
        for i, grad in enumerate((mm(ds, stacked(qf * inv), NN), mm(pb, stacked(uf * inv), NN))):
            acc[g, i] = grad[128:448].reshape(10, 2, 16, 128)
            zs[g, 0, i] = grad[0:128].astype(jnp.bfloat16)
            zs[g, 1, i] = grad[448:576].astype(jnp.bfloat16)

    def unpack(g, side, block):
        both = mm(unpacks[block], jnp.concatenate([zr[g, side, 0], zr[g, side, 1]], axis=1), NN)
        acc[g, 0, :, block] += both[:, 0:128].reshape(10, 16, 128)
        acc[g, 1, :, block] += both[:, 128:256].reshape(10, 16, 128)

    def stage_y(g):
        got(zgrad(g))

        @pl.when(has_hi)
        def _():
            unpack(g, 0, 1)

        @pl.when(has_lo)
        def _():
            unpack(g, 1, 0)

        ys[g, 0] = acc[g, :, 4:7].astype(jnp.bfloat16)
        ys[g, 1] = acc[g, :, 7:10].astype(jnp.bfloat16)
        start(ygrad(g))

    def stage_out(g):
        got(ygrad(g))

        @pl.when(has_r)
        def _():
            acc[g, :, 1:4] += yr[g, 0].astype(jnp.float32)

        @pl.when(has_l)
        def _():
            acc[g, :, 0:3] += yr[g, 1].astype(jnp.float32)

        for i, ref in enumerate((gk_ref, gv_ref)):
            own = acc[g, i, 0:4].reshape(128, 128).astype(jnp.bfloat16)
            put(ref, g, mm(perm, own, TN))

    AHEAD = 2
    for g in range(AHEAD):
        forward(g)

    def step(g, carry):
        @pl.when(g + AHEAD < G)
        def _():
            forward(g + AHEAD)

        @pl.when(g < G)
        def _():
            got(zmain(g))
            compute(g)
            start(zgrad(g))

        @pl.when((g >= 1) & (g < G + 1))
        def _():
            stage_y(g - 1)

        @pl.when(g >= 3)
        def _():
            stage_out(g - 3)

        return carry

    lax.fori_loop(0, G + 3, step, 0)

    def drain(g, carry):
        for copies in (ymain(g), zmain(g), zgrad(g), ygrad(g)):
            sent(copies)
        return carry

    lax.fori_loop(0, G, drain, 0)


def on_device(queries, key_field, value_field, upstream):
    shape = queries.shape
    pairs = shape[3] // 128
    vmem = pl.BlockSpec(memory_space=pltpu.VMEM)
    dma = lambda: pltpu.SemaphoreType.DMA((pairs, 2))
    outs = pl.pallas_call(
        functools.partial(kernel, lax.axis_size("space"), lax.axis_size("tp")),
        out_shape=[jax.ShapeDtypeStruct(shape, jnp.bfloat16)] * 4,
        in_specs=[vmem] * 4,
        out_specs=[vmem] * 4,
        scratch_shapes=[
            pltpu.VMEM((pairs, 2, 10, 2, 16, 128), jnp.bfloat16),
            pltpu.VMEM((pairs, 2, 2, 128, 128), jnp.bfloat16),
            pltpu.VMEM((pairs, 2, 2, 128, 128), jnp.bfloat16),
            pltpu.VMEM((576, 128), jnp.bfloat16),
            pltpu.VMEM((256, 128), jnp.bfloat16),
            pltpu.VMEM((pairs, 2, 10, 2, 16, 128), jnp.float32),
            pltpu.VMEM((pairs, 2, 2, 128, 128), jnp.bfloat16),
            pltpu.VMEM((pairs, 2, 2, 128, 128), jnp.bfloat16),
            pltpu.VMEM((pairs, 2, 2, 3, 2, 16, 128), jnp.bfloat16),
            pltpu.VMEM((pairs, 2, 2, 3, 2, 16, 128), jnp.bfloat16),
        ] + [dma() for _ in range(8)],
        compiler_params=pltpu.CompilerParams(
            collective_id=0, has_side_effects=True, vmem_limit_bytes=48 * 1024 * 1024
        ),
        cost_estimate=pl.CostEstimate(flops=2 * 10**9, bytes_accessed=4 * 10**6, transcendentals=10**6),
        name="window_attention",
    )(queries, key_field, value_field, upstream)
    return tuple(outs)


def solution(mesh):
    spec = P("space", "tp", None, None)
    return jax.shard_map(
        on_device, mesh=mesh, in_specs=(spec,) * 4, out_specs=(spec,) * 4, check_vma=False
    )
```

```python
import functools

import jax
import jax.numpy as jnp
from jax import lax
from jax.experimental import pallas as pl
from jax.experimental.pallas import tpu as pltpu
from jax.sharding import PartitionSpec as P

HEADS = 16
RADIUS = 3
BLOCKED = -1e30
MESH = pl.DeviceIdType.MESH
NT = (((1,), (1,)), ((), ()))
TN = (((0,), (0,)), ((), ()))
NN = (((1,), (0,)), ((), ()))


def mm(a, b, dims):
    return lax.dot_general(a, b, dims, preferred_element_type=jnp.float32)


def kernel(
    ns, nt, q_hbm, k_hbm, v_hbm, u_hbm, o_ref, gq_ref, gk_ref, gv_ref,
    q_ref, k_ref, v_ref, u_ref, kv, pack, rim, kmask, qmask, acc, zs, zr, ys, yr,
    ym_s, ym_r, z_s, z_r, zg_s, zg_r, yg_s, yg_r, zo_s, zo_r, zgo_s, zgo_r, in_s,
):
    G = kv.shape[0]
    si = lax.axis_index("space")
    ti = lax.axis_index("tp")
    has_lo, has_hi = si > 0, si < ns - 1
    has_l, has_r = ti > 0, ti < nt - 1
    lo, hi, left, right = (si - 1, ti), (si + 1, ti), (si, ti - 1), (si, ti + 1)

    loads = [
        pltpu.make_async_copy(src, dst, in_s.at[i])
        for i, (src, dst) in enumerate(((k_hbm, k_ref), (v_hbm, v_ref), (q_hbm, q_ref), (u_hbm, u_ref)))
    ]
    for load in loads:
        load.start()

    barrier = pltpu.get_barrier_semaphore()
    for have, dev in ((has_lo, lo), (has_hi, hi), (has_l, left), (has_r, right)):
        @pl.when(have)
        def _(dev=dev):
            pl.semaphore_signal(barrier, inc=1, device_id=dev, device_id_type=MESH)

    def remote(src, dst, ss, rs, dev):
        return pltpu.make_async_remote_copy(
            src_ref=src, dst_ref=dst, send_sem=ss, recv_sem=rs, device_id=dev, device_id_type=MESH
        )

    def ymain(g):
        return (
            (remote(kv.at[g, :, 0:3], kv.at[g, :, 7:10], ym_s.at[g, 0], ym_r.at[g, 0], left), has_l, has_r),
            (remote(kv.at[g, :, 1:4], kv.at[g, :, 4:7], ym_s.at[g, 1], ym_r.at[g, 1], right), has_r, has_l),
        )

    def along_z(src, dst, ss, rs, g, rows, flip):
        return tuple(
            (
                remote(src.at[g, i, :, rows], dst.at[g, 1 - i if flip else i, :, rows], ss.at[g, i], rs.at[g, i], dev),
                send,
                recv,
            )
            for i, dev, send, recv in ((0, lo, has_lo, has_hi), (1, hi, has_hi, has_lo))
        )

    own_rows, corner_rows = pl.ds(0, 48), pl.ds(48, 80)

    def zown(g):
        return along_z(pack, rim, zo_s, zo_r, g, own_rows, True)

    def zcorner(g):
        return along_z(pack, rim, z_s, z_r, g, corner_rows, True)

    def zgrad_own(g):
        return along_z(zs, zr, zgo_s, zgo_r, g, own_rows, False)

    def zgrad_corner(g):
        return along_z(zs, zr, zg_s, zg_r, g, corner_rows, False)

    def ygrad(g):
        return (
            (remote(ys.at[g, 0], yr.at[g, 0], yg_s.at[g, 0], yg_r.at[g, 0], left), has_l, has_r),
            (remote(ys.at[g, 1], yr.at[g, 1], yg_s.at[g, 1], yg_r.at[g, 1], right), has_r, has_l),
        )

    def start(copies):
        for c, send, _r in copies:
            @pl.when(send)
            def _(c=c):
                c.start()

    def got(copies):
        for c, _s, recv in copies:
            @pl.when(recv)
            def _(c=c):
                c.wait_recv()

    def sent(copies):
        for c, send, _r in copies:
            @pl.when(send)
            def _(c=c):
                c.wait_send()

    def lanes(g):
        return pl.ds(pl.multiple_of(g * 128, 128), 128)

    def iota(shape, dim):
        return lax.broadcasted_iota(jnp.int32, shape, dim)

    r = iota((224, 128), 0)
    t = jnp.where(r >= 176, r - 176, r - 128)
    x = jnp.where(r < 128, (r // 4) % 8, (t % 12) // 4 + jnp.where(r >= 176, 5, 0))
    y = jnp.where(r < 128, r // 32, t // 12)
    spread = jnp.where(iota((224, 128), 1) == x * 16 + y * 4 + r % 4, 1.0, 0.0).astype(jnp.bfloat16)
    r, c = iota((128, 128), 0), iota((128, 128), 1)
    perm = jnp.where(c == ((r // 4) % 8) * 16 + (r // 32) * 4 + r % 4, 1.0, 0.0).astype(jnp.bfloat16)

    barrier_count = (
        has_lo.astype(jnp.int32) + has_hi.astype(jnp.int32) + has_l.astype(jnp.int32) + has_r.astype(jnp.int32)
    )

    def choose(packed, cell, first, used):
        hit = (cell == (packed // 12) * 16 + packed % 12 + first) & (packed < used)
        return jnp.where(hit, 1.0, 0.0).astype(jnp.bfloat16)

    packs = [choose(iota((80, 96), 0), iota((80, 96), 1), 4 * i, 72) for i in range(2)]
    unpacks = [choose(iota((96, 80), 1), iota((96, 80), 0), 4 * i, 72) for i in range(2)]
    unpacks_own = [choose(iota((64, 48), 1), iota((64, 48), 0), 4 * i, 48) for i in range(2)]

    def cells(ref, g):
        return ref[:, :, :, lanes(g)].astype(jnp.float32).reshape(128, 128)

    def put(ref, g, x):
        ref[:, :, :, lanes(g)] = x.reshape(8, 4, 4, 128).astype(jnp.bfloat16)

    def fill(g):
        both = jnp.concatenate([cells(k_ref, g), cells(v_ref, g)], axis=1).astype(jnp.bfloat16)
        out = mm(spread, both, NN).astype(jnp.bfloat16)
        for i in range(2):
            part = out[:, 128 * i : 128 * i + 128]
            kv[g, i, 0:4] = part[0:128].reshape(4, 2, 16, 128)
            pack[g, 0, i, 0:48] = part[128:176]
            pack[g, 1, i, 0:48] = part[176:224]

    loads[0].wait()
    loads[1].wait()
    fill(0)
    pl.semaphore_wait(barrier, barrier_count)
    start(ymain(0))
    start(zown(0))

    def prologue(g, carry):
        fill(g)
        start(ymain(g))
        start(zown(g))
        return carry

    lax.fori_loop(1, G, prologue, 0)

    @pl.when(jnp.logical_not(has_l))
    def _():
        kv[:, :, 4:7] = jnp.zeros((G, 2, 3, 2, 16, 128), jnp.bfloat16)

    @pl.when(jnp.logical_not(has_r))
    def _():
        kv[:, :, 7:10] = jnp.zeros((G, 2, 3, 2, 16, 128), jnp.bfloat16)

    @pl.when(jnp.logical_not(has_lo))
    def _():
        rim[:, 0] = jnp.zeros((G, 2, 128, 128), jnp.bfloat16)

    @pl.when(jnp.logical_not(has_hi))
    def _():
        rim[:, 1] = jnp.zeros((G, 2, 128, 128), jnp.bfloat16)

    row, f = iota((576, 128), 0), iota((576, 128), 1)
    low, high = row < 128, row >= 448
    t = jnp.where(low, row, jnp.where(high, row - 448, row - 128))
    edge = low | high
    j = jnp.where(edge, t // 12, t // 32)
    spare = edge & (t >= 120)
    ky = jnp.where(j < 4, j, jnp.where(j < 7, j - 7, j - 3))
    kx = jnp.where(low, (t % 12) // 4 - 3, jnp.where(high, (t % 12) // 4 + 8, (t % 32) // 4))
    on = (spare & (f == 32)) | (jnp.logical_not(spare) & ((f == kx + 3) | (f == ky + 19)))
    kmask[...] = jnp.where(on, 1.0, 0.0).astype(jnp.bfloat16)

    col, f = iota((256, 128), 0) % 128, iota((256, 128), 1)
    qx, qy = col // 16, (col // 4) % 4
    kx, ky = f - 3, f - 19
    gx, gy = kx + si * 8, ky + ti * 4
    far_x = (jnp.abs(kx - qx) > RADIUS) | (gx < 0) | (gx >= ns * 8)
    far_y = (jnp.abs(ky - qy) > RADIUS) | (gy < 0) | (gy >= nt * 4)
    off = ((f < 14) & far_x) | ((f >= 16) & (f < 26) & far_y) | (f == 32)
    qmask[...] = jnp.where(off, BLOCKED, 0.0).astype(jnp.bfloat16)

    lane = lax.broadcasted_iota(jnp.int32, (128, 128), 1)
    feat = lax.broadcasted_iota(jnp.int32, (128, 128), 0)

    def stacked(x):
        zero = jnp.zeros_like(x)
        return jnp.concatenate([jnp.where(lane < 64, x, zero), jnp.where(lane >= 64, x, zero)], axis=0).astype(jnp.bfloat16)

    def diagonal(x):
        return jnp.where(feat < 64, x[:, 0:128], x[:, 128:256])

    def forward(g):
        got(ymain(g))
        for i in range(2):
            both = jnp.concatenate([kv[g, n, 4:10, i].reshape(96, 128) for n in range(2)], axis=1)
            out = mm(packs[i], both, NN).astype(jnp.bfloat16)
            pack[g, i, 0, 48:128] = out[:, 0:128]
            pack[g, i, 1, 48:128] = out[:, 128:256]
        start(zcorner(g))

    def compute(gs):
        def all_rows(g, i):
            return jnp.concatenate([rim[g, 0, i], kv[g, i].reshape(320, 128), rim[g, 1, i]], axis=0)

        both = range(len(gs))
        qf = [cells(q_ref, g) * 0.125 for g in gs]
        uf = [cells(u_ref, g) for g in gs]
        s = [
            mm(
                jnp.concatenate([all_rows(gs[n], 0), kmask[...]], axis=1),
                jnp.concatenate([stacked(qf[n]), qmask[...]], axis=1),
                NT,
            )
            for n in both
        ]
        dp, pb, p, inv, ds = {}, {}, {}, {}, {}
        for n in both:
            p[n] = jnp.exp(s[n] - jnp.max(s[n], axis=0, keepdims=True))
            total = 1.0 / jnp.sum(p[n], axis=0, keepdims=True)
            inv[n] = jnp.where(feat < 64, total[:, 0:128], total[:, 128:256])
            pb[n] = p[n].astype(jnp.bfloat16)
            dp[n] = mm(all_rows(gs[n], 1), stacked(uf[n]), NT)
        for n in both:
            ot = diagonal(mm(all_rows(gs[n], 1), pb[n], TN)) * inv[n]
            put(o_ref, gs[n], ot.T)
            prod = uf[n].T * ot.astype(jnp.bfloat16).astype(jnp.float32)
            dots = jnp.concatenate(
                [jnp.sum(prod[0:64], axis=0, keepdims=True), jnp.sum(prod[64:128], axis=0, keepdims=True)], axis=1
            )
            ds[n] = (p[n] * (dp[n] - dots)).astype(jnp.bfloat16)
        for n in both:
            g = gs[n]
            turned = inv[n].T
            for i, grad in enumerate((mm(ds[n], stacked(qf[n] * turned), NN), mm(pb[n], stacked(uf[n] * turned), NN))):
                acc[g, i] = grad[128:448].reshape(10, 2, 16, 128)
                zs[g, 0, i] = grad[0:128].astype(jnp.bfloat16)
                zs[g, 1, i] = grad[448:576].astype(jnp.bfloat16)
        for g in gs:
            start(zgrad_corner(g))
        for g in gs:
            start(zgrad_own(g))
        for n, g in enumerate(gs):
            put(gq_ref, g, (diagonal(mm(all_rows(g, 0), ds[n], TN)) * (inv[n] * 0.125)).T)

    def unpack(g, which, rows, first, last):
        for side, block, have in ((0, 1, has_hi), (1, 0, has_lo)):
            @pl.when(have)
            def _(side=side, block=block):
                both = mm(which[block], jnp.concatenate([zr[g, side, 0, rows], zr[g, side, 1, rows]], axis=1), NN)
                for n in range(2):
                    part = both[:, 128 * n : 128 * n + 128].reshape(last - first, 16, 128)
                    acc[g, n, first:last, block] += part

    def stage_y(g):
        got(zgrad_corner(g))
        unpack(g, unpacks, corner_rows, 4, 10)
        ys[g, 0] = acc[g, :, 4:7].astype(jnp.bfloat16)
        ys[g, 1] = acc[g, :, 7:10].astype(jnp.bfloat16)
        start(ygrad(g))

    def stage_out(g):
        got(zgrad_own(g))
        unpack(g, unpacks_own, own_rows, 0, 4)
        got(ygrad(g))

        @pl.when(has_r)
        def _():
            acc[g, :, 1:4] += yr[g, 0].astype(jnp.float32)

        @pl.when(has_l)
        def _():
            acc[g, :, 0:3] += yr[g, 1].astype(jnp.float32)

        for i, ref in enumerate((gk_ref, gv_ref)):
            own = acc[g, i, 0:4].reshape(128, 128).astype(jnp.bfloat16)
            put(ref, g, mm(perm, own, TN))

    H = G // 2
    loads[2].wait()
    loads[3].wait()
    forward(0)
    forward(1)

    def step(h, carry):
        @pl.when(h + 1 < H)
        def _():
            forward(2 * h + 2)
            forward(2 * h + 3)

        @pl.when(h < H)
        def _():
            for g in (2 * h, 2 * h + 1):
                got(zown(g))
                got(zcorner(g))
            compute((2 * h, 2 * h + 1))

        @pl.when((h >= 1) & (h < H + 1))
        def _():
            stage_y(2 * h - 2)
            stage_y(2 * h - 1)

        @pl.when(h >= 2)
        def _():
            stage_out(2 * h - 4)
            stage_out(2 * h - 3)

        return carry

    lax.fori_loop(0, H + 2, step, 0)

    def drain(g, carry):
        for copies in (ymain(g), zown(g), zcorner(g), zgrad_own(g), zgrad_corner(g), ygrad(g)):
            sent(copies)
        return carry

    lax.fori_loop(0, G, drain, 0)


def on_device(queries, key_field, value_field, upstream):
    shape = queries.shape
    pairs = shape[3] // 128
    vmem = pl.BlockSpec(memory_space=pltpu.VMEM)
    hbm = pl.BlockSpec(memory_space=pltpu.HBM)
    dma = lambda: pltpu.SemaphoreType.DMA((pairs, 2))
    outs = pl.pallas_call(
        functools.partial(kernel, lax.axis_size("space"), lax.axis_size("tp")),
        out_shape=[jax.ShapeDtypeStruct(shape, jnp.bfloat16)] * 4,
        in_specs=[hbm] * 4,
        out_specs=[vmem] * 4,
        scratch_shapes=[pltpu.VMEM(shape, jnp.bfloat16) for _ in range(4)] + [
            pltpu.VMEM((pairs, 2, 10, 2, 16, 128), jnp.bfloat16),
            pltpu.VMEM((pairs, 2, 2, 128, 128), jnp.bfloat16),
            pltpu.VMEM((pairs, 2, 2, 128, 128), jnp.bfloat16),
            pltpu.VMEM((576, 128), jnp.bfloat16),
            pltpu.VMEM((256, 128), jnp.bfloat16),
            pltpu.VMEM((pairs, 2, 10, 2, 16, 128), jnp.float32),
            pltpu.VMEM((pairs, 2, 2, 128, 128), jnp.bfloat16),
            pltpu.VMEM((pairs, 2, 2, 128, 128), jnp.bfloat16),
            pltpu.VMEM((pairs, 2, 2, 3, 2, 16, 128), jnp.bfloat16),
            pltpu.VMEM((pairs, 2, 2, 3, 2, 16, 128), jnp.bfloat16),
        ] + [dma() for _ in range(12)] + [pltpu.SemaphoreType.DMA((4,))],
        compiler_params=pltpu.CompilerParams(
            collective_id=0, has_side_effects=True
        ),
        cost_estimate=pl.CostEstimate(flops=2 * 10**9, bytes_accessed=4 * 10**6, transcendentals=10**6),
        name="window_attention",
    )(queries, key_field, value_field, upstream)
    return tuple(outs)


def solution(mesh):
    spec = P("space", "tp", None, None)
    return jax.shard_map(
        on_device, mesh=mesh, in_specs=(spec,) * 4, out_specs=(spec,) * 4, check_vma=False
    )
```
